32 devices in a mesh: dp: 8 (over z, y), tensor: 4 (over x, core).
Axes of the slice: x: 2, y: 2, z: 4, core: 2. Of those that a mesh axis runs over, the one named last changes fastest.
Arguments:
- residual: bfloat16 [512, 8192], P('tensor'), may hold values from -120 to 120
- hidden_cotangent: bfloat16 [512, 14336], P('tensor', 'dp'), may hold values from -6 to 6
- norm_gain: float32 [8192], replicated, may hold values from 0.1 to 1.9
- gate_weight: bfloat16 [14336, 8192], P('dp', 'tensor'), may hold values from -0.0625 to 0.0625
- up_weight: bfloat16 [14336, 8192], P('dp', 'tensor'), may hold values from -0.0625 to 0.0625
Outputs:
- input_grad: bfloat16 [512, 8192], P('dp', 'tensor')
- gate_grad: bfloat16 [14336, 8192], P('dp', 'tensor')
- up_grad: bfloat16 [14336, 8192], P('dp', 'tensor')
- gain_grad: float32 [8192], P('tensor')
The draws below stay inside these ranges and needn't reach their ends.
All inputs are finite; a program needn't handle non-finite values.
Results may differ from the reference program's by a relative error of at most 0.0085.
Values may be sent and summed in bfloat16 or wider, within the bound.
A program may use at most 192 MiB of HBM per device.

```python
import math
import jax
import jax.numpy as jnp
from jax import lax

D = 8192
FFW = 14336
TOKENS = 512


def draw_residual(key, part):
    key = jax.random.fold_in(key, 7)
    key_col, key_row, key_val = jax.random.split(key, 3)
    ramp = jnp.arange(D, dtype=jnp.float32) / D
    column = jnp.exp(jax.random.uniform(key_col, (D,), jnp.float32) * math.log(10.0) + 0.5 * math.log(3.0) * ramp)
    row_scale = jnp.exp(jax.random.uniform(key_row, (TOKENS, 1), jnp.float32, math.log(0.1), math.log(1.0)))
    values = jax.random.normal(key_val, (TOKENS, D), jnp.float32)
    values = jnp.clip(values, -5.0, 5.0)
    return (values * column * row_scale).astype(jnp.bfloat16)


def levels(rng, shape, cuts, least, high):
    level = 1.0
    for dim, blocks in cuts:
        draws = jax.random.uniform(jax.random.fold_in(jax.random.fold_in(rng, 6), dim), (blocks,), jnp.float32, least / len(cuts), high / len(cuts))
        level = level * jnp.repeat(jnp.exp(draws), shape[dim] // blocks).reshape((-1,) + (1,) * (len(shape) - 1 - dim))
    return level


def scatter_about(stream_key, shape, width, reach, cuts=(), kind=jnp.bfloat16):
    loudness = levels(stream_key, shape, cuts, -0.22, 0.18) if cuts else 1.0
    array = jax.random.normal(stream_key, shape, jnp.float32) * width * loudness
    return jnp.minimum(jnp.maximum(array, -reach), reach).astype(kind)


def setup_inputs(seed: int = 0) -> dict:
    keys = jax.random.split(jax.random.key(seed), 6)
    residual = draw_residual(jax.random.fold_in(keys[5], 71), 0)
    hidden_cotangent = scatter_about(keys[1], (TOKENS, FFW), 1.0, 6.0, ((0, 4), (1, 8)))
    norm_gain = jnp.clip(1.0 + 0.18 * jax.random.normal(keys[2], (D,), jnp.float32), 0.1, 1.9)
    gate_weight = scatter_about(keys[3], (FFW, D), D ** -0.5, 0.0625, ((0, 8), (1, 4)))
    up_weight = scatter_about(keys[4], (FFW, D), D ** -0.5, 0.0625, ((0, 8), (1, 4)))
    return {"residual": residual, "hidden_cotangent": hidden_cotangent, "norm_gain": norm_gain, "gate_weight": gate_weight, "up_weight": up_weight}


def reference(residual, hidden_cotangent, norm_gain, gate_weight, up_weight):
    resid_f = residual.astype(jnp.float32)
    inv_rms = lax.rsqrt(lax.optimization_barrier(jnp.mean(resid_f * resid_f, axis=-1, keepdims=True)) + 1e-05)
    normed = (resid_f * inv_rms * norm_gain).astype(jnp.bfloat16)
    gate = jnp.dot(normed, gate_weight.T, preferred_element_type=jnp.float32)
    up_proj = jnp.dot(normed, up_weight.T, preferred_element_type=jnp.float32)
    cot_f = hidden_cotangent.astype(jnp.float32)
    sig = jax.nn.sigmoid(gate)
    gate_delta = (cot_f * up_proj * sig * (1.0 + gate * (1.0 - sig))).astype(jnp.bfloat16)
    up_delta = (cot_f * gate * sig).astype(jnp.bfloat16)
    scale = TOKENS ** (-0.5)
    gate_grad = (jnp.dot(gate_delta.T, normed, preferred_element_type=jnp.float32) * scale).astype(jnp.bfloat16)
    up_grad = (jnp.dot(up_delta.T, normed, preferred_element_type=jnp.float32) * scale).astype(jnp.bfloat16)
    delta = (jnp.dot(gate_delta, gate_weight, preferred_element_type=jnp.float32) + jnp.dot(up_delta, up_weight, preferred_element_type=jnp.float32)).astype(jnp.bfloat16)
    delta_f = lax.optimization_barrier(delta).astype(jnp.float32)
    gain_grad = lax.optimization_barrier(jnp.sum(delta_f * resid_f * inv_rms, axis=0)) * scale
    coeff = lax.optimization_barrier(jnp.sum(norm_gain * delta_f * resid_f, axis=-1, keepdims=True)) / D
    input_grad = (inv_rms * norm_gain * delta_f - resid_f * (inv_rms * inv_rms * inv_rms) * coeff).astype(jnp.bfloat16)
    return (input_grad, gate_grad, up_grad, gain_grad)
```

```python
import jax
import jax.numpy as jnp
from jax import lax
from jax.sharding import PartitionSpec as P


def activate(gate, up_proj, cotangent):
    cot_f = cotangent.astype(jnp.float32)
    sig = jax.nn.sigmoid(gate)
    gate_delta = (cot_f * up_proj * sig * (1.0 + gate * (1.0 - sig))).astype(jnp.bfloat16)
    up_delta = (cot_f * gate * sig).astype(jnp.bfloat16)
    return (gate_delta, up_delta)


def right_product(left, weight):
    return lax.dot_general(
        left, weight, (((1,), (1,)), ((), ())), preferred_element_type=jnp.float32
    )


def left_product(left, right):
    return lax.dot_general(
        left, right, (((0,), (0,)), ((), ())), preferred_element_type=jnp.float32
    )


def scattered_sum(part, axis):
    n = lax.axis_size(axis)
    pieces = part.astype(jnp.bfloat16).reshape(n, part.shape[0] // n, part.shape[1])
    pieces = lax.all_to_all(pieces, axis, split_axis=0, concat_axis=0, tiled=True)
    return jnp.sum(pieces.astype(jnp.float32), axis=0)


def shards(residual, hidden_cotangent, norm_gain, gate_weight, up_weight):
    width = residual.shape[1]
    slice_width = gate_weight.shape[1]
    tokens = residual.shape[0]
    feat_resid = lax.all_to_all(residual, "tensor", split_axis=1, concat_axis=0, tiled=True)
    resid_f = residual.astype(jnp.float32)
    own_inv = lax.rsqrt(jnp.mean(resid_f * resid_f, axis=-1) + 1e-05)
    feat_inv = lax.all_gather(own_inv, "tensor", axis=0, tiled=True)[:, None]
    feat_f = feat_resid.astype(jnp.float32)
    gain_slice = lax.dynamic_slice_in_dim(
        norm_gain, lax.axis_index("tensor") * slice_width, slice_width
    )
    feat_normed = (feat_f * feat_inv * gain_slice).astype(jnp.bfloat16)
    gate = scattered_sum(right_product(feat_normed, gate_weight), "tensor")
    up_proj = scattered_sum(right_product(feat_normed, up_weight), "tensor")
    gate_delta, up_delta = activate(gate, up_proj, hidden_cotangent)
    gate_all, up_all = (
        lax.all_gather(gate_delta, "tensor", axis=0, tiled=True),
        lax.all_gather(up_delta, "tensor", axis=0, tiled=True),
    )
    tokens_total = tokens * lax.axis_size("tensor")
    scale = tokens_total ** (-0.5)
    rows_each = tokens_total // lax.axis_size("dp")
    delta_part = jnp.dot(gate_all, gate_weight, preferred_element_type=jnp.float32) + jnp.dot(
        up_all, up_weight, preferred_element_type=jnp.float32
    )
    delta_rows = scattered_sum(delta_part, "dp")
    gate_grad = (left_product(gate_all, feat_normed) * scale).astype(jnp.bfloat16)
    up_grad = (left_product(up_all, feat_normed) * scale).astype(jnp.bfloat16)
    delta_f = delta_rows.astype(jnp.bfloat16).astype(jnp.float32)
    row_start = lax.axis_index("dp") * rows_each
    resid_rows = lax.dynamic_slice_in_dim(feat_resid, row_start, rows_each, 0).astype(jnp.float32)
    inv_rows = lax.dynamic_slice_in_dim(feat_inv, row_start, rows_each, 0)
    gain_part = jnp.sum(delta_f * resid_rows * inv_rows, axis=0)
    coeff_part = jnp.sum(gain_slice * delta_f * resid_rows, axis=1)
    coeff = lax.psum(coeff_part, "tensor")[:, None] / width
    gain_total = lax.psum(gain_part, "dp")
    input_grad = (
        inv_rows * gain_slice * delta_f - resid_rows * (inv_rows * inv_rows * inv_rows) * coeff
    )
    return (input_grad.astype(jnp.bfloat16), gate_grad, up_grad, gain_total * scale)


def solution(mesh):
    return jax.shard_map(
        shards,
        mesh=mesh,
        in_specs=(P("tensor", None), P("tensor", "dp"), P(), P("dp", "tensor"), P("dp", "tensor")),
        out_specs=(P("dp", "tensor"), P("dp", "tensor"), P("dp", "tensor"), P("tensor")),
        check_vma=False,
    )
```

```python
import functools

import jax
import jax.numpy as jnp
from jax import lax
from jax.experimental import pallas as pl
from jax.experimental.pallas import tpu as pltpu
from jax.sharding import PartitionSpec as P


def activate(gate, up_proj, cotangent):
    cot_f = cotangent.astype(jnp.float32)
    sig = jax.nn.sigmoid(gate)
    gate_delta = (cot_f * up_proj * sig * (1.0 + gate * (1.0 - sig))).astype(jnp.bfloat16)
    up_delta = (cot_f * gate * sig).astype(jnp.bfloat16)
    return (gate_delta, up_delta)


def right_product(left, weight):
    return lax.dot_general(
        left, weight, (((1,), (1,)), ((), ())), preferred_element_type=jnp.float32
    )


def left_product(left, right):
    return lax.dot_general(
        left, right, (((0,), (0,)), ((), ())), preferred_element_type=jnp.float32
    )


def scattered_sum(part, axis):
    n = lax.axis_size(axis)
    pieces = part.astype(jnp.bfloat16).reshape(n, part.shape[0] // n, part.shape[1])
    pieces = lax.all_to_all(pieces, axis, split_axis=0, concat_axis=0, tiled=True)
    return jnp.sum(pieces.astype(jnp.float32), axis=0)


MESH = pl.DeviceIdType.MESH


def delta_kernel(
    groups, chunks, normed, cot, gate_w, up_w, gate_all, up_all,
    paired, weights, pair_out, pair_in, own, far_out, far_in,
    w_sem, pair_s, pair_r, far_s, far_r, peer_s, peer_r, sib_s, sib_r,
):
    me = lax.axis_index("tensor")
    dp = lax.axis_index("dp")
    core, group = lax.rem(me, 2), me // 2
    sib_core = 1 - core
    rows = cot.shape[0]
    half = groups * rows
    cols = cot.shape[1] // chunks
    sibling = (dp, group * 2 + sib_core)

    def other(j):
        return lax.rem(group + j, groups)

    def block(g, c):
        return pl.ds(pl.multiple_of((g * 2 + c) * rows, rows), rows)

    def span(k):
        return pl.ds(0, cols) if chunks == 1 else pl.ds(pl.multiple_of(k * cols, cols), cols)

    def w_copies(k):
        start = pl.ds(pl.multiple_of(k * cols, cols), cols)
        return [
            pltpu.make_async_copy(w.at[start], weights.at[k, pl.ds(i * cols, cols)], w_sem.at[k, i])
            for i, w in enumerate((gate_w, up_w))
        ]

    for k in range(chunks):
        for copy in w_copies(k):
            copy.start()

    barrier = pltpu.get_barrier_semaphore()
    pl.semaphore_signal(barrier, inc=1, device_id=sibling, device_id_type=MESH)
    for j in range(1, groups):
        pl.semaphore_signal(
            barrier, inc=1, device_id=(dp, other(j) * 2 + core), device_id_type=MESH
        )

    for g in range(groups):
        paired[pl.ds(g * rows, rows)] = normed[block(g, sib_core)]
        paired[pl.ds(half + g * rows, rows)] = normed[block(g, core)]
    pl.semaphore_wait(barrier, groups)

    def pair_copy(k):
        return pltpu.make_async_remote_copy(
            pair_out.at[k], pair_in.at[k], pair_s.at[k], pair_r.at[k],
            device_id=sibling, device_id_type=MESH,
        )

    def far_copy(k, j, source):
        return pltpu.make_async_remote_copy(
            far_out.at[k, j - 1], far_in.at[k, source], far_s.at[k, j - 1], far_r.at[k, source],
            device_id=(dp, other(j) * 2 + core), device_id_type=MESH,
        )

    def peer_copy(k, j, source, i):
        part = (gate_all, up_all)[i].at[block(source, core), span(k)]
        return pltpu.make_async_remote_copy(
            part, part, peer_s.at[k, j - 1, i], peer_r.at[k, source, i],
            device_id=(dp, other(j) * 2 + core), device_id_type=MESH,
        )

    def sib_copy(k, source, i, c):
        part = (gate_all, up_all)[i].at[block(source, c), span(k)]
        return pltpu.make_async_remote_copy(
            part, part, sib_s.at[k, source, i], sib_r.at[k, source, i],
            device_id=sibling, device_id_type=MESH,
        )

    def product(k):
        for copy in w_copies(k):
            copy.wait()
        part = right_product(paired[...], weights[k])
        pair_out[k] = part[:half].astype(jnp.bfloat16)
        own[k] = part[half:]
        pair_copy(k).start()

    def pair_sum(k):
        pair_copy(k).wait_recv()
        for j in range(1, groups):
            at = pl.ds(pl.multiple_of(other(j) * rows, rows), rows)
            total = own[k, at] + pair_in[k, at].astype(jnp.float32)
            far_out[k, j - 1] = total.astype(jnp.bfloat16)
            far_copy(k, j, group).start()

    def deltas(k):
        at = pl.ds(pl.multiple_of(group * rows, rows), rows)
        total = own[k, at] + pair_in[k, at].astype(jnp.float32)
        for j in range(1, groups):
            far_copy(k, j, other(j)).wait_recv()
            total += far_in[k, other(j)].astype(jnp.float32)
        gate_d, up_d = activate(total[:, :cols], total[:, cols:], cot[:, span(k)])
        gate_all[block(group, core), span(k)] = gate_d
        up_all[block(group, core), span(k)] = up_d
        for i in range(2):
            for j in range(1, groups):
                peer_copy(k, j, group, i).start()
            sib_copy(k, group, i, core).start()

    def forward(k):
        for j in range(1, groups):
            for i in range(2):
                peer_copy(k, j, other(j), i).wait_recv()
                sib_copy(k, other(j), i, core).start()

    stages = ((product, 0), (pair_sum, 1), (deltas, 3), (forward, 5))

    def step(s, carry):
        for stage, lag in stages:
            @pl.when((s >= lag) & (s < chunks + lag))
            def _():
                stage(s - lag)
        return carry

    lax.fori_loop(0, chunks + stages[-1][1], step, 0)

    def finish(k, carry):
        pair_copy(k).wait_send()
        for j in range(1, groups):
            far_copy(k, j, group).wait_send()
            for i in range(2):
                peer_copy(k, j, group, i).wait_send()
        for g in range(groups):
            for i in range(2):
                sib_copy(k, g, i, core).wait_send()
                sib_copy(k, g, i, sib_core).wait_recv()
        return carry

    lax.fori_loop(0, chunks, finish, 0)


def all_deltas(normed, cot, gate_weight, up_weight):
    rows, hidden = cot.shape
    total, width = normed.shape
    groups = total // rows // 2
    chunks = hidden // 256 if hidden % 256 == 0 else 1
    cols = hidden // chunks
    half = groups * rows
    dma = pltpu.SemaphoreType.DMA
    vmem = pl.BlockSpec(memory_space=pltpu.VMEM)
    flops = 4 * total * width * hidden
    return pl.pallas_call(
        functools.partial(delta_kernel, groups, chunks),
        out_shape=[jax.ShapeDtypeStruct((total, hidden), jnp.bfloat16)] * 2,
        in_specs=[vmem, vmem, pl.BlockSpec(memory_space=pl.ANY), pl.BlockSpec(memory_space=pl.ANY)],
        out_specs=[vmem, vmem],
        scratch_shapes=[
            pltpu.VMEM((total, width), jnp.bfloat16),
            pltpu.VMEM((chunks, 2 * cols, width), jnp.bfloat16),
            pltpu.VMEM((chunks, half, 2 * cols), jnp.bfloat16),
            pltpu.VMEM((chunks, half, 2 * cols), jnp.bfloat16),
            pltpu.VMEM((chunks, half, 2 * cols), jnp.float32),
            pltpu.VMEM((chunks, max(groups - 1, 1), rows, 2 * cols), jnp.bfloat16),
            pltpu.VMEM((chunks, groups, rows, 2 * cols), jnp.bfloat16),
            dma((chunks, 2)),
            dma((chunks,)),
            dma((chunks,)),
            dma((chunks, groups)),
            dma((chunks, groups)),
            dma((chunks, groups, 2)),
            dma((chunks, groups, 2)),
            dma((chunks, groups, 2)),
            dma((chunks, groups, 2)),
        ],
        compiler_params=pltpu.CompilerParams(
            collective_id=0, has_side_effects=True, vmem_limit_bytes=56 * 1024 * 1024
        ),
        cost_estimate=pl.CostEstimate(
            flops=flops, bytes_accessed=4 * hidden * width, transcendentals=0
        ),
    )(normed, cot, gate_weight, up_weight)


def shards(residual, hidden_cotangent, norm_gain, gate_weight, up_weight):
    width = residual.shape[1]
    slice_width = gate_weight.shape[1]
    tokens = residual.shape[0]
    feat_resid = lax.all_to_all(residual, "tensor", split_axis=1, concat_axis=0, tiled=True)
    resid_f = residual.astype(jnp.float32)
    own_inv = lax.rsqrt(jnp.mean(resid_f * resid_f, axis=-1) + 1e-05)
    feat_inv = lax.all_gather(own_inv, "tensor", axis=0, tiled=True)[:, None]
    feat_f = feat_resid.astype(jnp.float32)
    gain_slice = lax.dynamic_slice_in_dim(
        norm_gain, lax.axis_index("tensor") * slice_width, slice_width
    )
    feat_normed = (feat_f * feat_inv * gain_slice).astype(jnp.bfloat16)
    gate_all, up_all = all_deltas(feat_normed, hidden_cotangent, gate_weight, up_weight)
    tokens_total = tokens * lax.axis_size("tensor")
    scale = tokens_total ** (-0.5)
    rows_each = tokens_total // lax.axis_size("dp")
    delta_part = jnp.dot(gate_all, gate_weight, preferred_element_type=jnp.float32) + jnp.dot(
        up_all, up_weight, preferred_element_type=jnp.float32
    )
    delta_rows = scattered_sum(delta_part, "dp")
    gate_grad = (left_product(gate_all, feat_normed) * scale).astype(jnp.bfloat16)
    up_grad = (left_product(up_all, feat_normed) * scale).astype(jnp.bfloat16)
    delta_f = delta_rows.astype(jnp.bfloat16).astype(jnp.float32)
    row_start = lax.axis_index("dp") * rows_each
    resid_rows = lax.dynamic_slice_in_dim(feat_resid, row_start, rows_each, 0).astype(jnp.float32)
    inv_rows = lax.dynamic_slice_in_dim(feat_inv, row_start, rows_each, 0)
    gain_part = jnp.sum(delta_f * resid_rows * inv_rows, axis=0)
    coeff_part = jnp.sum(gain_slice * delta_f * resid_rows, axis=1)
    coeff = lax.psum(coeff_part, "tensor")[:, None] / width
    gain_total = lax.psum(gain_part, "dp")
    input_grad = (
        inv_rows * gain_slice * delta_f - resid_rows * (inv_rows * inv_rows * inv_rows) * coeff
    )
    return (input_grad.astype(jnp.bfloat16), gate_grad, up_grad, gain_total * scale)


def solution(mesh):
    return jax.shard_map(
        shards,
        mesh=mesh,
        in_specs=(P("tensor", None), P("tensor", "dp"), P(), P("dp", "tensor"), P("dp", "tensor")),
        out_specs=(P("dp", "tensor"), P("dp", "tensor"), P("dp", "tensor"), P("tensor")),
        check_vma=False,
    )
```

```python
import functools

import jax
import jax.numpy as jnp
from jax import lax
from jax.experimental import pallas as pl
from jax.experimental.pallas import tpu as pltpu
from jax.sharding import PartitionSpec as P


def activate(gate, up_proj, cotangent):
    cot_f = cotangent.astype(jnp.float32)
    sig = jax.nn.sigmoid(gate)
    gate_delta = (cot_f * up_proj * sig * (1.0 + gate * (1.0 - sig))).astype(jnp.bfloat16)
    up_delta = (cot_f * gate * sig).astype(jnp.bfloat16)
    return (gate_delta, up_delta)


def right_product(left, weight):
    return lax.dot_general(
        left, weight, (((1,), (1,)), ((), ())), preferred_element_type=jnp.float32
    )


def left_product(left, right):
    return lax.dot_general(
        left, right, (((0,), (0,)), ((), ())), preferred_element_type=jnp.float32
    )


MESH = pl.DeviceIdType.MESH


def delta_kernel(
    groups, chunks, normed, cot, gate_w, up_w, gate_all, up_all,
    paired, weights, pair_out, pair_in, own, far_out, far_in,
    w_sem, pair_s, pair_r, far_s, far_r, peer_s, peer_r, sib_s, sib_r,
):
    me = lax.axis_index("tensor")
    dp = lax.axis_index("dp")
    core, group = lax.rem(me, 2), me // 2
    sib_core = 1 - core
    rows = cot.shape[0]
    half = groups * rows
    cols = cot.shape[1] // chunks
    sibling = (dp, group * 2 + sib_core)

    def other(j):
        return lax.rem(group + j, groups)

    def block(g, c):
        return pl.ds(pl.multiple_of((g * 2 + c) * rows, rows), rows)

    def span(k):
        return pl.ds(0, cols) if chunks == 1 else pl.ds(pl.multiple_of(k * cols, cols), cols)

    def w_copies(k):
        start = pl.ds(pl.multiple_of(k * cols, cols), cols)
        return [
            pltpu.make_async_copy(w.at[start], weights.at[k, pl.ds(i * cols, cols)], w_sem.at[k, i])
            for i, w in enumerate((gate_w, up_w))
        ]

    for k in range(chunks):
        for copy in w_copies(k):
            copy.start()

    barrier = pltpu.get_barrier_semaphore()
    pl.semaphore_signal(barrier, inc=1, device_id=sibling, device_id_type=MESH)
    for j in range(1, groups):
        pl.semaphore_signal(
            barrier, inc=1, device_id=(dp, other(j) * 2 + core), device_id_type=MESH
        )

    for g in range(groups):
        paired[pl.ds(g * rows, rows)] = normed[block(g, sib_core)]
        paired[pl.ds(half + g * rows, rows)] = normed[block(g, core)]
    pl.semaphore_wait(barrier, groups)

    def pair_copy(k):
        return pltpu.make_async_remote_copy(
            pair_out.at[k], pair_in.at[k], pair_s.at[k], pair_r.at[k],
            device_id=sibling, device_id_type=MESH,
        )

    def far_copy(k, j, source):
        return pltpu.make_async_remote_copy(
            far_out.at[k, j - 1], far_in.at[k, source], far_s.at[k, j - 1], far_r.at[k, source],
            device_id=(dp, other(j) * 2 + core), device_id_type=MESH,
        )

    def peer_copy(k, j, source, i):
        part = (gate_all, up_all)[i].at[block(source, core), span(k)]
        return pltpu.make_async_remote_copy(
            part, part, peer_s.at[k, j - 1, i], peer_r.at[k, source, i],
            device_id=(dp, other(j) * 2 + core), device_id_type=MESH,
        )

    def sib_copy(k, source, i, c):
        part = (gate_all, up_all)[i].at[block(source, c), span(k)]
        return pltpu.make_async_remote_copy(
            part, part, sib_s.at[k, source, i], sib_r.at[k, source, i],
            device_id=sibling, device_id_type=MESH,
        )

    def product(k):
        for copy in w_copies(k):
            copy.wait()
        part = right_product(paired[...], weights[k])
        pair_out[k] = part[:half].astype(jnp.bfloat16)
        own[k] = part[half:]
        pair_copy(k).start()

    def pair_sum(k):
        pair_copy(k).wait_recv()
        for j in range(1, groups):
            at = pl.ds(pl.multiple_of(other(j) * rows, rows), rows)
            total = own[k, at] + pair_in[k, at].astype(jnp.float32)
            far_out[k, j - 1] = total.astype(jnp.bfloat16)
            far_copy(k, j, group).start()

    def deltas(k):
        at = pl.ds(pl.multiple_of(group * rows, rows), rows)
        total = own[k, at] + pair_in[k, at].astype(jnp.float32)
        for j in range(1, groups):
            far_copy(k, j, other(j)).wait_recv()
            total += far_in[k, other(j)].astype(jnp.float32)
        gate_d, up_d = activate(total[:, :cols], total[:, cols:], cot[:, span(k)])
        gate_all[block(group, core), span(k)] = gate_d
        up_all[block(group, core), span(k)] = up_d
        for i in range(2):
            for j in range(1, groups):
                peer_copy(k, j, group, i).start()
            sib_copy(k, group, i, core).start()

    def forward(k):
        for j in range(1, groups):
            for i in range(2):
                peer_copy(k, j, other(j), i).wait_recv()
                sib_copy(k, other(j), i, core).start()

    stages = ((product, 0), (pair_sum, 1), (deltas, 3), (forward, 5))

    def step(s, carry):
        for stage, lag in stages:
            @pl.when((s >= lag) & (s < chunks + lag))
            def _():
                stage(s - lag)
        return carry

    lax.fori_loop(0, chunks + stages[-1][1], step, 0)

    def finish(k, carry):
        pair_copy(k).wait_send()
        for j in range(1, groups):
            far_copy(k, j, group).wait_send()
            for i in range(2):
                peer_copy(k, j, group, i).wait_send()
        for g in range(groups):
            for i in range(2):
                sib_copy(k, g, i, core).wait_send()
                sib_copy(k, g, i, sib_core).wait_recv()
        return carry

    lax.fori_loop(0, chunks, finish, 0)


def all_deltas(normed, cot, gate_weight, up_weight):
    rows, hidden = cot.shape
    total, width = normed.shape
    groups = total // rows // 2
    chunks = hidden // 256 if hidden % 256 == 0 else 1
    cols = hidden // chunks
    half = groups * rows
    dma = pltpu.SemaphoreType.DMA
    vmem = pl.BlockSpec(memory_space=pltpu.VMEM)
    flops = 4 * total * width * hidden
    return pl.pallas_call(
        functools.partial(delta_kernel, groups, chunks),
        out_shape=[jax.ShapeDtypeStruct((total, hidden), jnp.bfloat16)] * 2,
        in_specs=[vmem, vmem, pl.BlockSpec(memory_space=pl.ANY), pl.BlockSpec(memory_space=pl.ANY)],
        out_specs=[vmem, vmem],
        scratch_shapes=[
            pltpu.VMEM((total, width), jnp.bfloat16),
            pltpu.VMEM((chunks, 2 * cols, width), jnp.bfloat16),
            pltpu.VMEM((chunks, half, 2 * cols), jnp.bfloat16),
            pltpu.VMEM((chunks, half, 2 * cols), jnp.bfloat16),
            pltpu.VMEM((chunks, half, 2 * cols), jnp.float32),
            pltpu.VMEM((chunks, max(groups - 1, 1), rows, 2 * cols), jnp.bfloat16),
            pltpu.VMEM((chunks, groups, rows, 2 * cols), jnp.bfloat16),
            dma((chunks, 2)),
            dma((chunks,)),
            dma((chunks,)),
            dma((chunks, groups)),
            dma((chunks, groups)),
            dma((chunks, groups, 2)),
            dma((chunks, groups, 2)),
            dma((chunks, groups, 2)),
            dma((chunks, groups, 2)),
        ],
        compiler_params=pltpu.CompilerParams(
            collective_id=0, has_side_effects=True, vmem_limit_bytes=56 * 1024 * 1024
        ),
        cost_estimate=pl.CostEstimate(
            flops=flops, bytes_accessed=4 * hidden * width, transcendentals=0
        ),
    )(normed, cot, gate_weight, up_weight)


def input_kernel(
    scale, gate_all, up_all, gate_w, up_w, resid, inv, gain, grad, gain_grad,
    paired, weights, pair_out, pair_in, own, far_out, far_in, delta, gain_in, coeff_in,
    w_sem, pair_s, pair_r, far_s, far_r, gain_s, gain_r, coeff_s, coeff_r,
):
    me = lax.axis_index("tensor")
    dp = lax.axis_index("dp")
    n_tensor, n_dp = coeff_in.shape[0], gain_in.shape[0]
    chunks, _, _, cols = weights.shape
    rows = resid.shape[0]
    groups = n_dp // 2
    half = groups * rows
    hidden = gate_w.shape[0]
    side, group = lax.rem(dp, 2), dp // 2
    mate = (group * 2 + 1 - side, me)

    def other(j):
        return lax.rem(group + j, groups)

    def dp_peer(j):
        return lax.rem(dp + j, n_dp)

    def tensor_peer(j):
        return lax.rem(me + j, n_tensor)

    def block(g, c):
        return pl.ds(pl.multiple_of((g * 2 + c) * rows, rows), rows)

    def span(m):
        return pl.ds(pl.multiple_of(m * cols, cols), cols)

    def w_copies(m):
        return [
            pltpu.make_async_copy(w.at[:, span(m)], weights.at[m, i], w_sem.at[m, i])
            for i, w in enumerate((gate_w, up_w))
        ]

    for m in range(chunks):
        for copy in w_copies(m):
            copy.start()

    barrier = pltpu.get_barrier_semaphore()
    for j in range(1, n_dp):
        pl.semaphore_signal(barrier, inc=1, device_id=(dp_peer(j), me), device_id_type=MESH)
    for j in range(1, n_tensor):
        pl.semaphore_signal(barrier, inc=1, device_id=(dp, tensor_peer(j)), device_id_type=MESH)

    for i, source in enumerate((gate_all, up_all)):
        for g in range(groups):
            paired[i, pl.ds(g * rows, rows)] = source[block(g, 1 - side)]
            paired[i, pl.ds(half + g * rows, rows)] = source[block(g, side)]
    pl.semaphore_wait(barrier, n_dp + n_tensor - 2)

    def pair_copy(m):
        return pltpu.make_async_remote_copy(
            pair_out.at[m], pair_in.at[m], pair_s.at[m], pair_r.at[m],
            device_id=mate, device_id_type=MESH,
        )

    def far_copy(m, j, source):
        return pltpu.make_async_remote_copy(
            far_out.at[m, j - 1], far_in.at[m, source], far_s.at[m, j - 1], far_r.at[m, source],
            device_id=(other(j) * 2 + side, me), device_id_type=MESH,
        )

    def gain_copy(j, source):
        return pltpu.make_async_remote_copy(
            gain_in.at[source], gain_in.at[source], gain_s.at[j - 1], gain_r.at[source],
            device_id=(dp_peer(j), me), device_id_type=MESH,
        )

    def coeff_copy(j, source):
        return pltpu.make_async_remote_copy(
            coeff_in.at[source], coeff_in.at[source], coeff_s.at[j - 1], coeff_r.at[source],
            device_id=(dp, tensor_peer(j)), device_id_type=MESH,
        )

    def product(m):
        for copy in w_copies(m):
            copy.wait()
        part = jnp.dot(paired[0], weights[m, 0], preferred_element_type=jnp.float32)
        part += jnp.dot(paired[1], weights[m, 1], preferred_element_type=jnp.float32)
        pair_out[m] = part[:half].astype(jnp.bfloat16)
        own[m] = part[half:]
        pair_copy(m).start()

    def pair_sum(m):
        pair_copy(m).wait_recv()
        for j in range(1, groups):
            at = pl.ds(pl.multiple_of(other(j) * rows, rows), rows)
            total = own[m, at] + pair_in[m, at].astype(jnp.float32)
            far_out[m, j - 1] = total.astype(jnp.bfloat16)
            far_copy(m, j, group).start()

    def far_sum(m):
        at = pl.ds(pl.multiple_of(group * rows, rows), rows)
        total = own[m, at] + pair_in[m, at].astype(jnp.float32)
        for j in range(1, groups):
            far_copy(m, j, other(j)).wait_recv()
            total += far_in[m, other(j)].astype(jnp.float32)
        total = total.astype(jnp.bfloat16).astype(jnp.float32)
        delta[m] = total
        moved = total * resid[:, span(m)].astype(jnp.float32)
        gain_in[dp, :, span(m)] = jnp.sum(moved * inv[...], axis=0, keepdims=True)
        terms = moved * gain[:, span(m)]
        coeff_in[me] += sum(terms[:, c : c + 128] for c in range(0, cols, 128))

    coeff_in[me] = jnp.zeros(coeff_in.shape[1:], jnp.float32)
    stages = ((product, 0), (pair_sum, 1), (far_sum, 3))

    def step(s, carry):
        for stage, lag in stages:
            @pl.when((s >= lag) & (s < chunks + lag))
            def _():
                stage(s - lag)
        return carry

    lax.fori_loop(0, chunks + stages[-1][1], step, 0)

    for j in range(1, n_tensor):
        coeff_copy(j, me).start()
    for j in range(1, n_dp):
        gain_copy(j, dp).start()
    for j in range(1, n_tensor):
        coeff_copy(j, tensor_peer(j)).wait_recv()
    lanes = coeff_in[0]
    for t in range(1, n_tensor):
        lanes += coeff_in[t]
    coeff = jnp.sum(lanes, axis=1, keepdims=True) / (n_tensor * chunks * cols)
    inv_v = inv[...]
    cubed = inv_v * inv_v * inv_v

    for m in range(chunks):
        at = pl.ds(m * cols, cols)
        grad[:, at] = (
            inv_v * gain[:, at] * delta[m] - resid[:, at].astype(jnp.float32) * cubed * coeff
        ).astype(grad.dtype)

    for j in range(1, n_dp):
        gain_copy(j, dp_peer(j)).wait_recv()
    total = gain_in[0]
    for d in range(1, n_dp):
        total += gain_in[d]
    gain_grad[...] = total * scale

    def finish(m, carry):
        pair_copy(m).wait_send()
        for j in range(1, groups):
            far_copy(m, j, group).wait_send()
        return carry

    lax.fori_loop(0, chunks, finish, 0)
    for j in range(1, n_tensor):
        coeff_copy(j, me).wait_send()
    for j in range(1, n_dp):
        gain_copy(j, dp).wait_send()


def input_gradient(gate_all, up_all, gate_weight, up_weight, resid_rows, inv_rows, gain, scale):
    total, hidden = gate_all.shape
    rows, width = resid_rows.shape
    n_dp, n_tensor = lax.axis_size("dp"), lax.axis_size("tensor")
    groups = n_dp // 2
    half = groups * rows
    cols = 256
    chunks = width // cols
    dma = pltpu.SemaphoreType.DMA
    vmem = pl.BlockSpec(memory_space=pltpu.VMEM)
    hbm = pl.BlockSpec(memory_space=pl.ANY)
    return pl.pallas_call(
        functools.partial(input_kernel, scale),
        out_shape=[
            jax.ShapeDtypeStruct((rows, width), jnp.bfloat16),
            jax.ShapeDtypeStruct((1, width), jnp.float32),
        ],
        in_specs=[vmem, vmem, hbm, hbm, vmem, vmem, vmem],
        out_specs=[vmem, vmem],
        scratch_shapes=[
            pltpu.VMEM((2, total, hidden), jnp.bfloat16),
            pltpu.VMEM((chunks, 2, hidden, cols), jnp.bfloat16),
            pltpu.VMEM((chunks, half, cols), jnp.bfloat16),
            pltpu.VMEM((chunks, half, cols), jnp.bfloat16),
            pltpu.VMEM((chunks, half, cols), jnp.float32),
            pltpu.VMEM((chunks, max(groups - 1, 1), rows, cols), jnp.bfloat16),
            pltpu.VMEM((chunks, groups, rows, cols), jnp.bfloat16),
            pltpu.VMEM((chunks, rows, cols), jnp.float32),
            pltpu.VMEM((n_dp, 1, width), jnp.float32),
            pltpu.VMEM((n_tensor, rows, 128), jnp.float32),
            dma((chunks, 2)),
            dma((chunks,)),
            dma((chunks,)),
            dma((chunks, groups)),
            dma((chunks, groups)),
            dma((n_dp,)),
            dma((n_dp,)),
            dma((n_tensor,)),
            dma((n_tensor,)),
        ],
        compiler_params=pltpu.CompilerParams(
            collective_id=1, has_side_effects=True, vmem_limit_bytes=56 * 1024 * 1024
        ),
        cost_estimate=pl.CostEstimate(
            flops=4 * total * width * hidden,
            bytes_accessed=4 * hidden * width,
            transcendentals=0,
        ),
    )(gate_all, up_all, gate_weight, up_weight, resid_rows, inv_rows, gain)


def shards(residual, hidden_cotangent, norm_gain, gate_weight, up_weight):
    width = residual.shape[1]
    slice_width = gate_weight.shape[1]
    tokens = residual.shape[0]
    feat_resid = lax.all_to_all(residual, "tensor", split_axis=1, concat_axis=0, tiled=True)
    resid_f = residual.astype(jnp.float32)
    own_inv = lax.rsqrt(jnp.mean(resid_f * resid_f, axis=-1) + 1e-05)
    feat_inv = lax.all_gather(own_inv, "tensor", axis=0, tiled=True)[:, None]
    feat_f = feat_resid.astype(jnp.float32)
    gain_slice = lax.dynamic_slice_in_dim(
        norm_gain, lax.axis_index("tensor") * slice_width, slice_width
    )
    feat_normed = (feat_f * feat_inv * gain_slice).astype(jnp.bfloat16)
    gate_all, up_all = all_deltas(feat_normed, hidden_cotangent, gate_weight, up_weight)
    tokens_total = tokens * lax.axis_size("tensor")
    scale = tokens_total ** (-0.5)
    rows_each = tokens_total // lax.axis_size("dp")
    gate_grad = (left_product(gate_all, feat_normed) * scale).astype(jnp.bfloat16)
    up_grad = (left_product(up_all, feat_normed) * scale).astype(jnp.bfloat16)
    row_start = lax.axis_index("dp") * rows_each
    resid_rows = lax.dynamic_slice_in_dim(feat_resid, row_start, rows_each, 0)
    inv_rows = lax.dynamic_slice_in_dim(feat_inv, row_start, rows_each, 0)
    input_grad, gain_grad = input_gradient(
        gate_all, up_all, gate_weight, up_weight, resid_rows, inv_rows, gain_slice[None], scale
    )
    return (input_grad, gate_grad, up_grad, gain_grad[0])


def solution(mesh):
    return jax.shard_map(
        shards,
        mesh=mesh,
        in_specs=(P("tensor", None), P("tensor", "dp"), P(), P("dp", "tensor"), P("dp", "tensor")),
        out_specs=(P("dp", "tensor"), P("dp", "tensor"), P("dp", "tensor"), P("tensor")),
        check_vma=False,
    )
```

```python
import functools

import jax
import jax.numpy as jnp
from jax import lax
from jax.experimental import pallas as pl
from jax.experimental.pallas import tpu as pltpu
from jax.sharding import PartitionSpec as P


def activate(gate, up_proj, cotangent):
    cot_f = cotangent.astype(jnp.float32)
    sig = jax.nn.sigmoid(gate)
    gate_delta = (cot_f * up_proj * sig * (1.0 + gate * (1.0 - sig))).astype(jnp.bfloat16)
    up_delta = (cot_f * gate * sig).astype(jnp.bfloat16)
    return (gate_delta, up_delta)


def right_product(left, weight):
    return lax.dot_general(
        left, weight, (((1,), (1,)), ((), ())), preferred_element_type=jnp.float32
    )


def left_product(left, right):
    return lax.dot_general(
        left, right, (((0,), (0,)), ((), ())), preferred_element_type=jnp.float32
    )


MESH = pl.DeviceIdType.MESH


def delta_kernel(
    groups, chunks, residual, all_gain, cot, gate_w, up_w, gate_all, up_all, normed, inv_all,
    norm_out, norm_s, norm_r, paired, weights, pair_out, pair_in, own, far_out, far_in,
    w_sem, pair_s, pair_r, far_s, far_r, peer_s, peer_r, sib_s, sib_r,
):
    me = lax.axis_index("tensor")
    dp = lax.axis_index("dp")
    core, group = lax.rem(me, 2), me // 2
    sib_core = 1 - core
    rows = cot.shape[0]
    half = groups * rows
    cols = cot.shape[1] // chunks
    sibling = (dp, group * 2 + sib_core)

    def other(j):
        return lax.rem(group + j, groups)

    def block(g, c):
        return pl.ds(pl.multiple_of((g * 2 + c) * rows, rows), rows)

    def span(k):
        return pl.ds(0, cols) if chunks == 1 else pl.ds(pl.multiple_of(k * cols, cols), cols)

    def w_copies(k):
        start = pl.ds(pl.multiple_of(k * cols, cols), cols)
        return [
            pltpu.make_async_copy(w.at[start], weights.at[k, pl.ds(i * cols, cols)], w_sem.at[k, i])
            for i, w in enumerate((gate_w, up_w))
        ]

    for k in range(chunks):
        for copy in w_copies(k):
            copy.start()

    barrier = pltpu.get_barrier_semaphore()
    pl.semaphore_signal(barrier, inc=1, device_id=sibling, device_id_type=MESH)
    for j in range(1, groups):
        pl.semaphore_signal(
            barrier, inc=1, device_id=(dp, other(j) * 2 + core), device_id_type=MESH
        )
        pl.semaphore_signal(
            barrier, inc=1, device_id=(dp, other(j) * 2 + sib_core), device_id_type=MESH
        )

    n_tensor, _, width = norm_out.shape
    squares = jnp.zeros((rows, 1), jnp.float32)
    for p in range(n_tensor):
        part = residual[:, pl.ds(p * width, width)].astype(jnp.float32)
        squares += jnp.sum(part * part, axis=1, keepdims=True)
    inv = lax.rsqrt(squares / (n_tensor * width) + 1e-05)
    for p in range(n_tensor):
        at = pl.ds(p * width, width)
        norm_out[p] = (residual[:, at].astype(jnp.float32) * inv * all_gain[:, at]).astype(
            jnp.bfloat16
        )
    normed[block(group, core)] = norm_out[me]
    inv_all[block(group, core)] = jnp.broadcast_to(inv, (rows, 128))
    pl.semaphore_wait(barrier, n_tensor - 1)

    def norm_copies(j, source):
        peer = lax.rem(me + j, n_tensor)
        at = pl.ds(pl.multiple_of(source * rows, rows), rows)
        return [
            pltpu.make_async_remote_copy(
                part, whole.at[at], norm_s.at[j - 1, i], norm_r.at[source, i],
                device_id=(dp, peer), device_id_type=MESH,
            )
            for i, (part, whole) in enumerate(
                ((norm_out.at[peer], normed), (inv_all.at[at], inv_all))
            )
        ]

    for i in range(2):
        for j in range(1, n_tensor):
            norm_copies(j, me)[i].start()
    for j in range(1, n_tensor):
        norm_copies(j, lax.rem(me + j, n_tensor))[0].wait_recv()

    for g in range(groups):
        paired[pl.ds(g * rows, rows)] = normed[block(g, sib_core)]
        paired[pl.ds(half + g * rows, rows)] = normed[block(g, core)]

    def pair_copy(k):
        return pltpu.make_async_remote_copy(
            pair_out.at[k], pair_in.at[k], pair_s.at[k], pair_r.at[k],
            device_id=sibling, device_id_type=MESH,
        )

    def far_copy(k, j, source):
        return pltpu.make_async_remote_copy(
            far_out.at[k, j - 1], far_in.at[k, source], far_s.at[k, j - 1], far_r.at[k, source],
            device_id=(dp, other(j) * 2 + core), device_id_type=MESH,
        )

    def peer_copy(k, j, source, i):
        part = (gate_all, up_all)[i].at[block(source, core), span(k)]
        return pltpu.make_async_remote_copy(
            part, part, peer_s.at[k, j - 1, i], peer_r.at[k, source, i],
            device_id=(dp, other(j) * 2 + core), device_id_type=MESH,
        )

    def sib_copy(k, source, i, c):
        part = (gate_all, up_all)[i].at[block(source, c), span(k)]
        return pltpu.make_async_remote_copy(
            part, part, sib_s.at[k, source, i], sib_r.at[k, source, i],
            device_id=sibling, device_id_type=MESH,
        )

    def product(k):
        for copy in w_copies(k):
            copy.wait()
        part = right_product(paired[...], weights[k])
        pair_out[k] = part[:half].astype(jnp.bfloat16)
        own[k] = part[half:]
        pair_copy(k).start()

    def pair_sum(k):
        pair_copy(k).wait_recv()
        for j in range(1, groups):
            at = pl.ds(pl.multiple_of(other(j) * rows, rows), rows)
            total = own[k, at] + pair_in[k, at].astype(jnp.float32)
            far_out[k, j - 1] = total.astype(jnp.bfloat16)
            far_copy(k, j, group).start()

    def deltas(k):
        at = pl.ds(pl.multiple_of(group * rows, rows), rows)
        total = own[k, at] + pair_in[k, at].astype(jnp.float32)
        for j in range(1, groups):
            far_copy(k, j, other(j)).wait_recv()
            total += far_in[k, other(j)].astype(jnp.float32)
        gate_d, up_d = activate(total[:, :cols], total[:, cols:], cot[:, span(k)])
        gate_all[block(group, core), span(k)] = gate_d
        up_all[block(group, core), span(k)] = up_d
        for i in range(2):
            for j in range(1, groups):
                peer_copy(k, j, group, i).start()
            sib_copy(k, group, i, core).start()

    def forward(k):
        for j in range(1, groups):
            for i in range(2):
                peer_copy(k, j, other(j), i).wait_recv()
                sib_copy(k, other(j), i, core).start()

    stages = ((product, 0), (pair_sum, 1), (deltas, 3), (forward, 5))

    def step(s, carry):
        for stage, lag in stages:
            @pl.when((s >= lag) & (s < chunks + lag))
            def _():
                stage(s - lag)
        return carry

    lax.fori_loop(0, chunks + stages[-1][1], step, 0)

    def finish(k, carry):
        pair_copy(k).wait_send()
        for j in range(1, groups):
            far_copy(k, j, group).wait_send()
            for i in range(2):
                peer_copy(k, j, group, i).wait_send()
        for g in range(groups):
            for i in range(2):
                sib_copy(k, g, i, core).wait_send()
                sib_copy(k, g, i, sib_core).wait_recv()
        return carry

    lax.fori_loop(0, chunks, finish, 0)
    for j in range(1, n_tensor):
        norm_copies(j, lax.rem(me + j, n_tensor))[1].wait_recv()
        for copy in norm_copies(j, me):
            copy.wait_send()


def all_deltas(residual, gain, cot, gate_weight, up_weight):
    rows, hidden = cot.shape
    width = gate_weight.shape[1]
    n_tensor = lax.axis_size("tensor")
    total = rows * n_tensor
    groups = total // rows // 2
    chunks = hidden // 256 if hidden % 256 == 0 else 1
    cols = hidden // chunks
    half = groups * rows
    dma = pltpu.SemaphoreType.DMA
    vmem = pl.BlockSpec(memory_space=pltpu.VMEM)
    flops = 4 * total * width * hidden
    return pl.pallas_call(
        functools.partial(delta_kernel, groups, chunks),
        out_shape=[jax.ShapeDtypeStruct((total, hidden), jnp.bfloat16)] * 2
        + [
            jax.ShapeDtypeStruct((total, width), jnp.bfloat16),
            jax.ShapeDtypeStruct((total, 128), jnp.float32),
        ],
        in_specs=[vmem, vmem, vmem, pl.BlockSpec(memory_space=pl.ANY), pl.BlockSpec(memory_space=pl.ANY)],
        out_specs=[vmem] * 4,
        scratch_shapes=[
            pltpu.VMEM((n_tensor, rows, width), jnp.bfloat16),
            dma((n_tensor, 2)),
            dma((n_tensor, 2)),
            pltpu.VMEM((total, width), jnp.bfloat16),
            pltpu.VMEM((chunks, 2 * cols, width), jnp.bfloat16),
            pltpu.VMEM((chunks, half, 2 * cols), jnp.bfloat16),
            pltpu.VMEM((chunks, half, 2 * cols), jnp.bfloat16),
            pltpu.VMEM((chunks, half, 2 * cols), jnp.float32),
            pltpu.VMEM((chunks, max(groups - 1, 1), rows, 2 * cols), jnp.bfloat16),
            pltpu.VMEM((chunks, groups, rows, 2 * cols), jnp.bfloat16),
            dma((chunks, 2)),
            dma((chunks,)),
            dma((chunks,)),
            dma((chunks, groups)),
            dma((chunks, groups)),
            dma((chunks, groups, 2)),
            dma((chunks, groups, 2)),
            dma((chunks, groups, 2)),
            dma((chunks, groups, 2)),
        ],
        compiler_params=pltpu.CompilerParams(
            collective_id=0, has_side_effects=True, vmem_limit_bytes=56 * 1024 * 1024
        ),
        cost_estimate=pl.CostEstimate(
            flops=flops, bytes_accessed=4 * hidden * width, transcendentals=0
        ),
    )(residual, gain, cot, gate_weight, up_weight)


def input_kernel(
    scale, gate_all, up_all, gate_w, up_w, normed, inv, gain, grad, gain_grad,
    paired, weights, pair_out, pair_in, own, far_out, far_in, delta, gain_in, coeff_in,
    w_sem, pair_s, pair_r, far_s, far_r, gain_s, gain_r, coeff_s, coeff_r,
):
    me = lax.axis_index("tensor")
    dp = lax.axis_index("dp")
    n_tensor, n_dp = coeff_in.shape[0], gain_in.shape[0]
    chunks, _, _, cols = weights.shape
    rows = normed.shape[0]
    groups = n_dp // 2
    half = groups * rows
    hidden = gate_w.shape[0]
    side, group = lax.rem(dp, 2), dp // 2
    mate = (group * 2 + 1 - side, me)

    def other(j):
        return lax.rem(group + j, groups)

    def dp_peer(j):
        return lax.rem(dp + j, n_dp)

    def tensor_peer(j):
        return lax.rem(me + j, n_tensor)

    def block(g, c):
        return pl.ds(pl.multiple_of((g * 2 + c) * rows, rows), rows)

    def span(m):
        return pl.ds(pl.multiple_of(m * cols, cols), cols)

    def w_copies(m):
        return [
            pltpu.make_async_copy(w.at[:, span(m)], weights.at[m, i], w_sem.at[m, i])
            for i, w in enumerate((gate_w, up_w))
        ]

    for m in range(chunks):
        for copy in w_copies(m):
            copy.start()

    barrier = pltpu.get_barrier_semaphore()
    for j in range(1, n_dp):
        pl.semaphore_signal(barrier, inc=1, device_id=(dp_peer(j), me), device_id_type=MESH)
    for j in range(1, n_tensor):
        pl.semaphore_signal(barrier, inc=1, device_id=(dp, tensor_peer(j)), device_id_type=MESH)

    for i, source in enumerate((gate_all, up_all)):
        for g in range(groups):
            paired[i, pl.ds(g * rows, rows)] = source[block(g, 1 - side)]
            paired[i, pl.ds(half + g * rows, rows)] = source[block(g, side)]
    pl.semaphore_wait(barrier, n_dp + n_tensor - 2)

    def pair_copy(m):
        return pltpu.make_async_remote_copy(
            pair_out.at[m], pair_in.at[m], pair_s.at[m], pair_r.at[m],
            device_id=mate, device_id_type=MESH,
        )

    def far_copy(m, j, source):
        return pltpu.make_async_remote_copy(
            far_out.at[m, j - 1], far_in.at[m, source], far_s.at[m, j - 1], far_r.at[m, source],
            device_id=(other(j) * 2 + side, me), device_id_type=MESH,
        )

    def gain_copy(j, source):
        return pltpu.make_async_remote_copy(
            gain_in.at[source], gain_in.at[source], gain_s.at[j - 1], gain_r.at[source],
            device_id=(dp_peer(j), me), device_id_type=MESH,
        )

    def coeff_copy(j, source):
        return pltpu.make_async_remote_copy(
            coeff_in.at[source], coeff_in.at[source], coeff_s.at[j - 1], coeff_r.at[source],
            device_id=(dp, tensor_peer(j)), device_id_type=MESH,
        )

    def product(m):
        for copy in w_copies(m):
            copy.wait()
        part = jnp.dot(paired[0], weights[m, 0], preferred_element_type=jnp.float32)
        part += jnp.dot(paired[1], weights[m, 1], preferred_element_type=jnp.float32)
        pair_out[m] = part[:half].astype(jnp.bfloat16)
        own[m] = part[half:]
        pair_copy(m).start()

    def pair_sum(m):
        pair_copy(m).wait_recv()
        for j in range(1, groups):
            at = pl.ds(pl.multiple_of(other(j) * rows, rows), rows)
            total = own[m, at] + pair_in[m, at].astype(jnp.float32)
            far_out[m, j - 1] = total.astype(jnp.bfloat16)
            far_copy(m, j, group).start()

    def far_sum(m):
        at = pl.ds(pl.multiple_of(group * rows, rows), rows)
        total = own[m, at] + pair_in[m, at].astype(jnp.float32)
        for j in range(1, groups):
            far_copy(m, j, other(j)).wait_recv()
            total += far_in[m, other(j)].astype(jnp.float32)
        total = total.astype(jnp.bfloat16).astype(jnp.float32)
        delta[m] = total
        terms = total * normed[:, span(m)].astype(jnp.float32)
        gain_in[dp, :, span(m)] = jnp.sum(terms, axis=0, keepdims=True) / gain[:, span(m)]
        coeff_in[me] += sum(terms[:, c : c + 128] for c in range(0, cols, 128))

    coeff_in[me] = jnp.zeros(coeff_in.shape[1:], jnp.float32)
    stages = ((product, 0), (pair_sum, 1), (far_sum, 3))

    def step(s, carry):
        for stage, lag in stages:
            @pl.when((s >= lag) & (s < chunks + lag))
            def _():
                stage(s - lag)
        return carry

    lax.fori_loop(0, chunks + stages[-1][1], step, 0)

    for j in range(1, n_tensor):
        coeff_copy(j, me).start()
    for j in range(1, n_dp):
        gain_copy(j, dp).start()
    for j in range(1, n_tensor):
        coeff_copy(j, tensor_peer(j)).wait_recv()
    lanes = coeff_in[0]
    for t in range(1, n_tensor):
        lanes += coeff_in[t]
    coeff = jnp.sum(lanes, axis=1, keepdims=True) / (n_tensor * chunks * cols)
    inv_v = inv[:, :1]

    for m in range(chunks):
        at = pl.ds(m * cols, cols)
        grad[:, at] = (
            inv_v * (gain[:, at] * delta[m] - normed[:, at].astype(jnp.float32) / gain[:, at] * coeff)
        ).astype(grad.dtype)

    for j in range(1, n_dp):
        gain_copy(j, dp_peer(j)).wait_recv()
    total = gain_in[0]
    for d in range(1, n_dp):
        total += gain_in[d]
    gain_grad[...] = total * scale

    def finish(m, carry):
        pair_copy(m).wait_send()
        for j in range(1, groups):
            far_copy(m, j, group).wait_send()
        return carry

    lax.fori_loop(0, chunks, finish, 0)
    for j in range(1, n_tensor):
        coeff_copy(j, me).wait_send()
    for j in range(1, n_dp):
        gain_copy(j, dp).wait_send()


def input_gradient(gate_all, up_all, gate_weight, up_weight, normed_rows, inv_rows, gain, scale):
    total, hidden = gate_all.shape
    rows, width = normed_rows.shape
    n_dp, n_tensor = lax.axis_size("dp"), lax.axis_size("tensor")
    groups = n_dp // 2
    half = groups * rows
    cols = 256
    chunks = width // cols
    dma = pltpu.SemaphoreType.DMA
    vmem = pl.BlockSpec(memory_space=pltpu.VMEM)
    hbm = pl.BlockSpec(memory_space=pl.ANY)
    return pl.pallas_call(
        functools.partial(input_kernel, scale),
        out_shape=[
            jax.ShapeDtypeStruct((rows, width), jnp.bfloat16),
            jax.ShapeDtypeStruct((1, width), jnp.float32),
        ],
        in_specs=[vmem, vmem, hbm, hbm, vmem, vmem, vmem],
        out_specs=[vmem, vmem],
        scratch_shapes=[
            pltpu.VMEM((2, total, hidden), jnp.bfloat16),
            pltpu.VMEM((chunks, 2, hidden, cols), jnp.bfloat16),
            pltpu.VMEM((chunks, half, cols), jnp.bfloat16),
            pltpu.VMEM((chunks, half, cols), jnp.bfloat16),
            pltpu.VMEM((chunks, half, cols), jnp.float32),
            pltpu.VMEM((chunks, max(groups - 1, 1), rows, cols), jnp.bfloat16),
            pltpu.VMEM((chunks, groups, rows, cols), jnp.bfloat16),
            pltpu.VMEM((chunks, rows, cols), jnp.float32),
            pltpu.VMEM((n_dp, 1, width), jnp.float32),
            pltpu.VMEM((n_tensor, rows, 128), jnp.float32),
            dma((chunks, 2)),
            dma((chunks,)),
            dma((chunks,)),
            dma((chunks, groups)),
            dma((chunks, groups)),
            dma((n_dp,)),
            dma((n_dp,)),
            dma((n_tensor,)),
            dma((n_tensor,)),
        ],
        compiler_params=pltpu.CompilerParams(
            collective_id=1, has_side_effects=True, vmem_limit_bytes=56 * 1024 * 1024
        ),
        cost_estimate=pl.CostEstimate(
            flops=4 * total * width * hidden,
            bytes_accessed=4 * hidden * width,
            transcendentals=0,
        ),
    )(gate_all, up_all, gate_weight, up_weight, normed_rows, inv_rows, gain)


def shards(residual, hidden_cotangent, norm_gain, gate_weight, up_weight):
    slice_width = gate_weight.shape[1]
    tokens = residual.shape[0]
    gain_slice = lax.dynamic_slice_in_dim(
        norm_gain, lax.axis_index("tensor") * slice_width, slice_width
    )
    gate_all, up_all, feat_normed, feat_inv = all_deltas(
        residual, norm_gain[None], hidden_cotangent, gate_weight, up_weight
    )
    tokens_total = tokens * lax.axis_size("tensor")
    scale = tokens_total ** (-0.5)
    rows_each = tokens_total // lax.axis_size("dp")
    gate_grad = (left_product(gate_all, feat_normed) * scale).astype(jnp.bfloat16)
    up_grad = (left_product(up_all, feat_normed) * scale).astype(jnp.bfloat16)
    row_start = lax.axis_index("dp") * rows_each
    normed_rows = lax.dynamic_slice_in_dim(feat_normed, row_start, rows_each, 0)
    inv_rows = lax.dynamic_slice_in_dim(feat_inv, row_start, rows_each, 0)
    input_grad, gain_grad = input_gradient(
        gate_all, up_all, gate_weight, up_weight, normed_rows, inv_rows, gain_slice[None], scale
    )
    return (input_grad, gate_grad, up_grad, gain_grad[0])


def solution(mesh):
    return jax.shard_map(
        shards,
        mesh=mesh,
        in_specs=(P("tensor", None), P("tensor", "dp"), P(), P("dp", "tensor"), P("dp", "tensor")),
        out_specs=(P("dp", "tensor"), P("dp", "tensor"), P("dp", "tensor"), P("tensor")),
        check_vma=False,
    )
```

```python
import functools

import jax
import jax.numpy as jnp
from jax import lax
from jax.experimental import pallas as pl
from jax.experimental.pallas import tpu as pltpu
from jax.sharding import PartitionSpec as P


def activate(gate, up_proj, cotangent):
    cot_f = cotangent.astype(jnp.float32)
    sig = jax.nn.sigmoid(gate)
    gate_delta = (cot_f * up_proj * sig * (1.0 + gate * (1.0 - sig))).astype(jnp.bfloat16)
    up_delta = (cot_f * gate * sig).astype(jnp.bfloat16)
    return (gate_delta, up_delta)


def right_product(left, weight):
    return lax.dot_general(
        left, weight, (((1,), (1,)), ((), ())), preferred_element_type=jnp.float32
    )


def left_product(left, right):
    return lax.dot_general(
        left, right, (((0,), (0,)), ((), ())), preferred_element_type=jnp.float32
    )


MESH = pl.DeviceIdType.MESH


def delta_kernel(
    groups, chunks, residual, all_gain, cot, gate_w, up_w, gate_all, up_all, normed, inv_all,
    norm_out, norm_s, norm_r, paired, weights, pair_out, pair_in, own, far_out, far_in,
    w_sem, pair_s, pair_r, far_s, far_r, peer_s, peer_r, sib_s, sib_r,
):
    me = lax.axis_index("tensor")
    dp = lax.axis_index("dp")
    core, group = lax.rem(me, 2), me // 2
    sib_core = 1 - core
    rows = cot.shape[0]
    half = groups * rows
    cols = cot.shape[1] // chunks
    sibling = (dp, group * 2 + sib_core)

    def other(j):
        return lax.rem(group + j, groups)

    def block(g, c):
        return pl.ds(pl.multiple_of((g * 2 + c) * rows, rows), rows)

    def span(k):
        return pl.ds(0, cols) if chunks == 1 else pl.ds(pl.multiple_of(k * cols, cols), cols)

    def w_copies(k):
        start = pl.ds(pl.multiple_of(k * cols, cols), cols)
        return [
            pltpu.make_async_copy(w.at[start], weights.at[k, pl.ds(i * cols, cols)], w_sem.at[k, i])
            for i, w in enumerate((gate_w, up_w))
        ]

    for k in range(chunks):
        for copy in w_copies(k):
            copy.start()

    barrier = pltpu.get_barrier_semaphore()
    pl.semaphore_signal(barrier, inc=1, device_id=sibling, device_id_type=MESH)
    for j in range(1, groups):
        pl.semaphore_signal(
            barrier, inc=1, device_id=(dp, other(j) * 2 + core), device_id_type=MESH
        )
        pl.semaphore_signal(
            barrier, inc=1, device_id=(dp, other(j) * 2 + sib_core), device_id_type=MESH
        )

    n_tensor, _, width = norm_out.shape
    squares = jnp.zeros((rows, 1), jnp.float32)
    for p in range(n_tensor):
        part = residual[:, pl.ds(p * width, width)].astype(jnp.float32)
        squares += jnp.sum(part * part, axis=1, keepdims=True)
    inv = lax.rsqrt(squares / (n_tensor * width) + 1e-05)

    def normalize(p):
        at = pl.ds(pl.multiple_of(p * width, width), width)
        return (residual[:, at].astype(jnp.float32) * inv * all_gain[:, at]).astype(jnp.bfloat16)

    inv_all[me] = jnp.transpose(jnp.broadcast_to(inv, (rows, 128)))[:8]
    pl.semaphore_wait(barrier, n_tensor - 1)

    def norm_copies(j, source):
        peer = lax.rem(me + j, n_tensor)
        at = pl.ds(pl.multiple_of(source * rows, rows), rows)
        return [
            pltpu.make_async_remote_copy(
                part, whole, norm_s.at[j - 1, i], norm_r.at[source, i],
                device_id=(dp, peer), device_id_type=MESH,
            )
            for i, (part, whole) in enumerate(
                ((norm_out.at[peer], normed.at[at]), (inv_all.at[source], inv_all.at[source]))
            )
        ]

    for j in sorted(range(1, n_tensor), key=lambda j: abs(2 * j - n_tensor)):
        peer = lax.rem(me + j, n_tensor)
        norm_out[peer] = normalize(peer)
        norm_copies(j, me)[0].start()
    normed[block(group, core)] = normalize(me)
    for j in range(1, n_tensor):
        norm_copies(j, me)[1].start()
    for j in range(1, n_tensor):
        norm_copies(j, lax.rem(me + j, n_tensor))[0].wait_recv()

    for g in range(groups):
        paired[pl.ds(g * rows, rows)] = normed[block(g, sib_core)]
        paired[pl.ds(half + g * rows, rows)] = normed[block(g, core)]

    def pair_copy(k):
        return pltpu.make_async_remote_copy(
            pair_out.at[k], pair_in.at[k], pair_s.at[k], pair_r.at[k],
            device_id=sibling, device_id_type=MESH,
        )

    def far_copy(k, j, source):
        return pltpu.make_async_remote_copy(
            far_out.at[k, j - 1], far_in.at[k, source], far_s.at[k, j - 1], far_r.at[k, source],
            device_id=(dp, other(j) * 2 + core), device_id_type=MESH,
        )

    def peer_copy(k, j, source, i):
        part = (gate_all, up_all)[i].at[block(source, core), span(k)]
        return pltpu.make_async_remote_copy(
            part, part, peer_s.at[k, j - 1, i], peer_r.at[k, source, i],
            device_id=(dp, other(j) * 2 + core), device_id_type=MESH,
        )

    def sib_copy(k, source, i, c):
        part = (gate_all, up_all)[i].at[block(source, c), span(k)]
        return pltpu.make_async_remote_copy(
            part, part, sib_s.at[k, source, i], sib_r.at[k, source, i],
            device_id=sibling, device_id_type=MESH,
        )

    def product(k):
        for copy in w_copies(k):
            copy.wait()
        part = right_product(paired[...], weights[k])
        pair_out[k] = part[:half].astype(jnp.bfloat16)
        own[k] = part[half:]
        pair_copy(k).start()

    def pair_sum(k):
        pair_copy(k).wait_recv()
        for j in range(1, groups):
            at = pl.ds(pl.multiple_of(other(j) * rows, rows), rows)
            total = own[k, at] + pair_in[k, at].astype(jnp.float32)
            far_out[k, j - 1] = total.astype(jnp.bfloat16)
            far_copy(k, j, group).start()

    def deltas(k):
        at = pl.ds(pl.multiple_of(group * rows, rows), rows)
        total = own[k, at] + pair_in[k, at].astype(jnp.float32)
        for j in range(1, groups):
            far_copy(k, j, other(j)).wait_recv()
            total += far_in[k, other(j)].astype(jnp.float32)
        gate_d, up_d = activate(total[:, :cols], total[:, cols:], cot[:, span(k)])
        gate_all[block(group, core), span(k)] = gate_d
        up_all[block(group, core), span(k)] = up_d
        for i in range(2):
            for j in range(1, groups):
                peer_copy(k, j, group, i).start()
            sib_copy(k, group, i, core).start()

    def forward(k):
        for j in range(1, groups):
            for i in range(2):
                peer_copy(k, j, other(j), i).wait_recv()
                sib_copy(k, other(j), i, core).start()

    stages = ((product, 0), (pair_sum, 1), (deltas, 3), (forward, 5))

    def step(s, carry):
        for stage, lag in stages:
            @pl.when((s >= lag) & (s < chunks + lag))
            def _():
                stage(s - lag)
        return carry

    lax.fori_loop(0, chunks + stages[-1][1], step, 0)

    def finish(k, carry):
        pair_copy(k).wait_send()
        for j in range(1, groups):
            far_copy(k, j, group).wait_send()
            for i in range(2):
                peer_copy(k, j, group, i).wait_send()
        for g in range(groups):
            for i in range(2):
                sib_copy(k, g, i, core).wait_send()
                sib_copy(k, g, i, sib_core).wait_recv()
        return carry

    lax.fori_loop(0, chunks, finish, 0)
    for j in range(1, n_tensor):
        norm_copies(j, lax.rem(me + j, n_tensor))[1].wait_recv()
        for copy in norm_copies(j, me):
            copy.wait_send()


def all_deltas(residual, gain, cot, gate_weight, up_weight):
    rows, hidden = cot.shape
    width = gate_weight.shape[1]
    n_tensor = lax.axis_size("tensor")
    total = rows * n_tensor
    groups = total // rows // 2
    chunks = hidden // 256 if hidden % 256 == 0 else 1
    cols = hidden // chunks
    half = groups * rows
    dma = pltpu.SemaphoreType.DMA
    vmem = pl.BlockSpec(memory_space=pltpu.VMEM)
    flops = 4 * total * width * hidden
    return pl.pallas_call(
        functools.partial(delta_kernel, groups, chunks),
        out_shape=[jax.ShapeDtypeStruct((total, hidden), jnp.bfloat16)] * 2
        + [
            jax.ShapeDtypeStruct((total, width), jnp.bfloat16),
            jax.ShapeDtypeStruct((n_tensor, 8, rows), jnp.float32),
        ],
        in_specs=[vmem, vmem, vmem, pl.BlockSpec(memory_space=pl.ANY), pl.BlockSpec(memory_space=pl.ANY)],
        out_specs=[vmem] * 4,
        scratch_shapes=[
            pltpu.VMEM((n_tensor, rows, width), jnp.bfloat16),
            dma((n_tensor, 2)),
            dma((n_tensor, 2)),
            pltpu.VMEM((total, width), jnp.bfloat16),
            pltpu.VMEM((chunks, 2 * cols, width), jnp.bfloat16),
            pltpu.VMEM((chunks, half, 2 * cols), jnp.bfloat16),
            pltpu.VMEM((chunks, half, 2 * cols), jnp.bfloat16),
            pltpu.VMEM((chunks, half, 2 * cols), jnp.float32),
            pltpu.VMEM((chunks, max(groups - 1, 1), rows, 2 * cols), jnp.bfloat16),
            pltpu.VMEM((chunks, groups, rows, 2 * cols), jnp.bfloat16),
            dma((chunks, 2)),
            dma((chunks,)),
            dma((chunks,)),
            dma((chunks, groups)),
            dma((chunks, groups)),
            dma((chunks, groups, 2)),
            dma((chunks, groups, 2)),
            dma((chunks, groups, 2)),
            dma((chunks, groups, 2)),
        ],
        compiler_params=pltpu.CompilerParams(
            collective_id=0, has_side_effects=True, vmem_limit_bytes=56 * 1024 * 1024
        ),
        cost_estimate=pl.CostEstimate(
            flops=flops, bytes_accessed=4 * hidden * width, transcendentals=0
        ),
    )(residual, gain, cot, gate_weight, up_weight)


def input_kernel(
    scale, gate_all, up_all, gate_w, up_w, normed, inv, gain, grad, gain_grad,
    paired, weights, pair_out, pair_in, own, far_out, far_in, delta, gain_in, coeff_in,
    w_sem, pair_s, pair_r, far_s, far_r, gain_s, gain_r, coeff_s, coeff_r,
):
    me = lax.axis_index("tensor")
    dp = lax.axis_index("dp")
    n_tensor, n_dp = coeff_in.shape[0], gain_in.shape[0]
    chunks, _, _, cols = weights.shape
    rows = normed.shape[0]
    groups = n_dp // 2
    half = groups * rows
    hidden = gate_w.shape[0]
    side, group = lax.rem(dp, 2), dp // 2
    mate = (group * 2 + 1 - side, me)

    def other(j):
        return lax.rem(group + j, groups)

    def dp_peer(j):
        return lax.rem(dp + j, n_dp)

    def tensor_peer(j):
        return lax.rem(me + j, n_tensor)

    def block(g, c):
        return pl.ds(pl.multiple_of((g * 2 + c) * rows, rows), rows)

    def span(m):
        return pl.ds(pl.multiple_of(m * cols, cols), cols)

    def w_copies(m):
        return [
            pltpu.make_async_copy(w.at[:, span(m)], weights.at[m, i], w_sem.at[m, i])
            for i, w in enumerate((gate_w, up_w))
        ]

    for m in range(chunks):
        for copy in w_copies(m):
            copy.start()

    barrier = pltpu.get_barrier_semaphore()
    for j in range(1, n_dp):
        pl.semaphore_signal(barrier, inc=1, device_id=(dp_peer(j), me), device_id_type=MESH)
    for j in range(1, n_tensor):
        pl.semaphore_signal(barrier, inc=1, device_id=(dp, tensor_peer(j)), device_id_type=MESH)

    for i, source in enumerate((gate_all, up_all)):
        for g in range(groups):
            paired[i, pl.ds(g * rows, rows)] = source[block(g, 1 - side)]
            paired[i, pl.ds(half + g * rows, rows)] = source[block(g, side)]
    pl.semaphore_wait(barrier, n_dp + n_tensor - 2)

    def pair_copy(m):
        return pltpu.make_async_remote_copy(
            pair_out.at[m], pair_in.at[m], pair_s.at[m], pair_r.at[m],
            device_id=mate, device_id_type=MESH,
        )

    def far_copy(m, j, source):
        return pltpu.make_async_remote_copy(
            far_out.at[m, j - 1], far_in.at[m, source], far_s.at[m, j - 1], far_r.at[m, source],
            device_id=(other(j) * 2 + side, me), device_id_type=MESH,
        )

    def gain_copy(j, source):
        return pltpu.make_async_remote_copy(
            gain_in.at[source], gain_in.at[source], gain_s.at[j - 1], gain_r.at[source],
            device_id=(dp_peer(j), me), device_id_type=MESH,
        )

    def coeff_copy(j, source):
        return pltpu.make_async_remote_copy(
            coeff_in.at[source], coeff_in.at[source], coeff_s.at[j - 1], coeff_r.at[source],
            device_id=(dp, tensor_peer(j)), device_id_type=MESH,
        )

    def product(m):
        for copy in w_copies(m):
            copy.wait()
        part = jnp.dot(paired[0], weights[m, 0], preferred_element_type=jnp.float32)
        part += jnp.dot(paired[1], weights[m, 1], preferred_element_type=jnp.float32)
        pair_out[m] = part[:half].astype(jnp.bfloat16)
        own[m] = part[half:]
        pair_copy(m).start()

    def pair_sum(m):
        pair_copy(m).wait_recv()
        for j in range(1, groups):
            at = pl.ds(pl.multiple_of(other(j) * rows, rows), rows)
            total = own[m, at] + pair_in[m, at].astype(jnp.float32)
            far_out[m, j - 1] = total.astype(jnp.bfloat16)
            far_copy(m, j, group).start()

    def far_sum(m):
        at = pl.ds(pl.multiple_of(group * rows, rows), rows)
        total = own[m, at] + pair_in[m, at].astype(jnp.float32)
        for j in range(1, groups):
            far_copy(m, j, other(j)).wait_recv()
            total += far_in[m, other(j)].astype(jnp.float32)
        total = total.astype(jnp.bfloat16).astype(jnp.float32)
        delta[m] = total
        terms = total * normed[:, span(m)].astype(jnp.float32)
        gain_in[dp, :, span(m)] = jnp.sum(terms, axis=0, keepdims=True) / gain[:, span(m)]
        coeff_in[me] += sum(terms[:, c : c + 128] for c in range(0, cols, 128))

    coeff_in[me] = jnp.zeros(coeff_in.shape[1:], jnp.float32)
    stages = ((product, 0), (pair_sum, 1), (far_sum, 3))

    def step(s, carry):
        for stage, lag in stages:
            @pl.when((s >= lag) & (s < chunks + lag))
            def _():
                stage(s - lag)
        return carry

    lax.fori_loop(0, chunks + stages[-1][1], step, 0)

    for j in range(1, n_tensor):
        coeff_copy(j, me).start()
    for j in range(1, n_dp):
        gain_copy(j, dp).start()
    for j in range(1, n_tensor):
        coeff_copy(j, tensor_peer(j)).wait_recv()
    lanes = coeff_in[0]
    for t in range(1, n_tensor):
        lanes += coeff_in[t]
    coeff = jnp.sum(lanes, axis=1, keepdims=True) / (n_tensor * chunks * cols)
    inv_v = inv[:, :1]

    for m in range(chunks):
        at = pl.ds(m * cols, cols)
        grad[:, at] = (
            inv_v * (gain[:, at] * delta[m] - normed[:, at].astype(jnp.float32) / gain[:, at] * coeff)
        ).astype(grad.dtype)

    for j in range(1, n_dp):
        gain_copy(j, dp_peer(j)).wait_recv()
    total = gain_in[0]
    for d in range(1, n_dp):
        total += gain_in[d]
    gain_grad[...] = total * scale

    def finish(m, carry):
        pair_copy(m).wait_send()
        for j in range(1, groups):
            far_copy(m, j, group).wait_send()
        return carry

    lax.fori_loop(0, chunks, finish, 0)
    for j in range(1, n_tensor):
        coeff_copy(j, me).wait_send()
    for j in range(1, n_dp):
        gain_copy(j, dp).wait_send()


def input_gradient(gate_all, up_all, gate_weight, up_weight, normed_rows, inv_rows, gain, scale):
    total, hidden = gate_all.shape
    rows, width = normed_rows.shape
    n_dp, n_tensor = lax.axis_size("dp"), lax.axis_size("tensor")
    groups = n_dp // 2
    half = groups * rows
    cols = 256
    chunks = width // cols
    dma = pltpu.SemaphoreType.DMA
    vmem = pl.BlockSpec(memory_space=pltpu.VMEM)
    hbm = pl.BlockSpec(memory_space=pl.ANY)
    return pl.pallas_call(
        functools.partial(input_kernel, scale),
        out_shape=[
            jax.ShapeDtypeStruct((rows, width), jnp.bfloat16),
            jax.ShapeDtypeStruct((1, width), jnp.float32),
        ],
        in_specs=[vmem, vmem, hbm, hbm, vmem, vmem, vmem],
        out_specs=[vmem, vmem],
        scratch_shapes=[
            pltpu.VMEM((2, total, hidden), jnp.bfloat16),
            pltpu.VMEM((chunks, 2, hidden, cols), jnp.bfloat16),
            pltpu.VMEM((chunks, half, cols), jnp.bfloat16),
            pltpu.VMEM((chunks, half, cols), jnp.bfloat16),
            pltpu.VMEM((chunks, half, cols), jnp.float32),
            pltpu.VMEM((chunks, max(groups - 1, 1), rows, cols), jnp.bfloat16),
            pltpu.VMEM((chunks, groups, rows, cols), jnp.bfloat16),
            pltpu.VMEM((chunks, rows, cols), jnp.float32),
            pltpu.VMEM((n_dp, 1, width), jnp.float32),
            pltpu.VMEM((n_tensor, rows, 128), jnp.float32),
            dma((chunks, 2)),
            dma((chunks,)),
            dma((chunks,)),
            dma((chunks, groups)),
            dma((chunks, groups)),
            dma((n_dp,)),
            dma((n_dp,)),
            dma((n_tensor,)),
            dma((n_tensor,)),
        ],
        compiler_params=pltpu.CompilerParams(
            collective_id=1, has_side_effects=True, vmem_limit_bytes=56 * 1024 * 1024
        ),
        cost_estimate=pl.CostEstimate(
            flops=4 * total * width * hidden,
            bytes_accessed=4 * hidden * width,
            transcendentals=0,
        ),
    )(gate_all, up_all, gate_weight, up_weight, normed_rows, inv_rows, gain)


def shards(residual, hidden_cotangent, norm_gain, gate_weight, up_weight):
    slice_width = gate_weight.shape[1]
    tokens = residual.shape[0]
    gain_slice = lax.dynamic_slice_in_dim(
        norm_gain, lax.axis_index("tensor") * slice_width, slice_width
    )
    gate_all, up_all, feat_normed, feat_inv = all_deltas(
        residual, norm_gain[None], hidden_cotangent, gate_weight, up_weight
    )
    feat_inv = feat_inv[:, 0].reshape(-1, 1)
    tokens_total = tokens * lax.axis_size("tensor")
    scale = tokens_total ** (-0.5)
    rows_each = tokens_total // lax.axis_size("dp")
    gate_grad = (left_product(gate_all, feat_normed) * scale).astype(jnp.bfloat16)
    up_grad = (left_product(up_all, feat_normed) * scale).astype(jnp.bfloat16)
    row_start = lax.axis_index("dp") * rows_each
    normed_rows = lax.dynamic_slice_in_dim(feat_normed, row_start, rows_each, 0)
    inv_rows = lax.dynamic_slice_in_dim(feat_inv, row_start, rows_each, 0)
    input_grad, gain_grad = input_gradient(
        gate_all, up_all, gate_weight, up_weight, normed_rows, inv_rows, gain_slice[None], scale
    )
    return (input_grad, gate_grad, up_grad, gain_grad[0])


def solution(mesh):
    return jax.shard_map(
        shards,
        mesh=mesh,
        in_specs=(P("tensor", None), P("tensor", "dp"), P(), P("dp", "tensor"), P("dp", "tensor")),
        out_specs=(P("dp", "tensor"), P("dp", "tensor"), P("dp", "tensor"), P("tensor")),
        check_vma=False,
    )
```
